32 devices in a mesh: dom: 8 (over z, x), bal: 4 (over y, core).
Axes of the slice: x: 2, y: 2, z: 4, core: 2. Of those that a mesh axis runs over, the one named last changes fastest.
Arguments:
- right_side: float32 [256, 64, 128], P(('dom', 'bal')), may hold values from -100 to 100
- a_tiles: bfloat16 [256, 5, 128, 128], P(('dom', 'bal')), may hold values from -4 to 4
- a_cols: int32 [256, 5], P(('dom', 'bal')), may hold values from 0 to 255, as said below
- m_tiles: bfloat16 [3328, 128, 128], P(('dom', 'bal')), may hold values from -2 to 2
- m_rows: int32 [3328], P(('dom', 'bal')), may hold values from 0 to 255, as said below
- m_cols: int32 [3328], P(('dom', 'bal')), may hold values from 0 to 255, as said below
- m_count: int32 [32], P(('dom', 'bal')), may hold values from 24 to 104, as said below
Outputs:
- solution: float32 [256, 64, 128], P(('dom', 'bal'))
- residual: float32 [256, 64, 128], P(('dom', 'bal'))
- basis: float32 [256, 64, 128], P(('dom', 'bal'))
- shadow: float32 [256, 64, 128], P(('dom', 'bal'))
The draws below stay inside these ranges and needn't reach their ends.
Inputs may be any that keep to these rules, and one draw needn't show every extreme that they name: a_cols[r, j] differs from r by at most 16, and every block row has a tile exactly 16 away. `m_rows`: the slots i * 104 to (i + 1) * 104 - 1 name block rows i * 8 to (i + 1) * 8 - 1, the rows of device i in the order of dom then bal. m_cols[s] differs from m_rows[s] by at most 32; on every device a live slot reaches exactly 32. The live slots of device i are its first m_count[i]; in every draw some device has all 104 live.
All inputs are finite; a program needn't handle non-finite values.
Results may differ from the reference program's by a relative error of at most 0.014.
Values may be sent and summed in bfloat16 or wider, within the bound.
A program may use at most 64 MiB of HBM per device.

```python
import math
import jax
import jax.numpy as jnp
from jax import lax

BR_DEV = 8
TILE = 128
NRHS = 64
KA = 5
MKEEP = 13
ITERS = 2
REACH_A = 16
REACH_M = 32
TILE_DEV = 104
NB = 256
MT = 3328


def draw_right_side(key, part):
    key_one, key_two = jax.random.split(key, 2)
    position = (jnp.arange(NB, dtype=jnp.float32)[:, None, None] * TILE + jnp.arange(TILE, dtype=jnp.float32)[None, None, :]) / (NB * TILE)
    column = jnp.exp(jax.random.uniform(key_two, (1, NRHS, 1), jnp.float32, math.log(0.3), math.log(3.0)))
    noise = jnp.clip(jax.random.normal(key_one, (NB, NRHS, TILE), jnp.float32), -4.0, 4.0)
    return noise * jnp.exp(position * math.log(3.0)) * column


def draw_a_tiles(key, part):
    key_one, key_two = jax.random.split(key)
    scale = 0.6 / math.sqrt(KA * TILE)
    noise = jnp.clip(jax.random.normal(key_one, (NB, KA, TILE, TILE), jnp.float32), -4.0, 4.0) * scale
    diag_vals = 1.5 + 1.5 * jax.random.uniform(key_two, (NB, 1, 1, TILE), jnp.float32)
    eye_mask = (jnp.arange(TILE)[:, None] == jnp.arange(TILE)[None, :]).astype(jnp.float32)
    first_slot = (jnp.arange(KA) == 0).astype(jnp.float32)[None, :, None, None]
    return (noise + first_slot * eye_mask[None, None] * diag_vals).astype(jnp.bfloat16)


def draw_a_cols(key, part):
    row_ids = jnp.arange(NB, dtype=jnp.int32)[:, None]
    offset = jax.random.randint(key, (NB, KA), -REACH_A, REACH_A + 1, dtype=jnp.int32)
    far_offset = jnp.where(row_ids + REACH_A < NB, REACH_A, -REACH_A)
    slot_ids = jnp.arange(KA, dtype=jnp.int32)[None, :]
    offset = jnp.where(slot_ids == 0, 0, jnp.where(slot_ids == 1, far_offset, offset))
    return jnp.clip(row_ids + offset, 0, NB - 1).astype(jnp.int32)


def tile_places(key):
    inner = jax.random.fold_in(key, 11)
    key_rows, key_cols = jax.random.split(inner)
    slot_ids = jnp.arange(MT, dtype=jnp.int32)
    owner_ids = slot_ids // TILE_DEV
    within = slot_ids % TILE_DEV
    spare_rows = jax.random.randint(key_rows, (MT,), 0, BR_DEV, dtype=jnp.int32)
    row_ids = owner_ids * BR_DEV + jnp.where(within < BR_DEV, within, spare_rows)
    offset = jax.random.randint(key_cols, (MT,), -REACH_M, REACH_M + 1, dtype=jnp.int32)
    far_offset = jnp.where(row_ids + REACH_M < NB, REACH_M, -REACH_M)
    offset = jnp.where(within < BR_DEV, 0, jnp.where(within == BR_DEV, far_offset, offset))
    col_ids = jnp.clip(row_ids + offset, 0, NB - 1)
    return (row_ids.astype(jnp.int32), col_ids.astype(jnp.int32))


def draw_m_rows(key, part):
    return tile_places(key)[0]


def draw_m_cols(key, part):
    return tile_places(key)[1]


def draw_m_tiles(key, part):
    key_one, key_two = jax.random.split(key)
    scale = 0.25 / math.sqrt(MKEEP * TILE)
    noise = jnp.clip(jax.random.normal(key_one, (MT, TILE, TILE), jnp.float32), -4.0, 4.0) * scale
    within = (jnp.arange(MT) % TILE_DEV)[:, None, None]
    diag_vals = 0.8 + 0.4 * jax.random.uniform(key_two, (MT, 1, TILE), jnp.float32)
    eye_mask = (jnp.arange(TILE)[:, None] == jnp.arange(TILE)[None, :]).astype(jnp.float32)
    return (noise + jnp.where(within < BR_DEV, 1.0, 0.0) * eye_mask[None] * diag_vals).astype(jnp.bfloat16)


def draw_m_count(key, part):
    key_one, key_two = jax.random.split(key)
    devices = NB // BR_DEV
    counts = jax.random.randint(key_one, (devices,), 3 * BR_DEV, 7 * BR_DEV + 1, dtype=jnp.int32)
    chosen = jax.random.randint(key_two, (), 0, devices, dtype=jnp.int32)
    return jnp.where(jnp.arange(devices, dtype=jnp.int32) == chosen, TILE_DEV, counts).astype(jnp.int32)


def setup_inputs(seed: int = 0) -> dict:
    seeds = jax.random.split(jax.random.key(seed), 8)
    return {
        "right_side": draw_right_side(jax.random.fold_in(seeds[7], 71), 0),
        "a_tiles": draw_a_tiles(jax.random.fold_in(seeds[7], 71), 0),
        "a_cols": draw_a_cols(jax.random.fold_in(seeds[7], 71), 0),
        "m_tiles": draw_m_tiles(jax.random.fold_in(seeds[7], 71), 0),
        "m_rows": draw_m_rows(jax.random.fold_in(seeds[7], 71), 0),
        "m_cols": draw_m_cols(jax.random.fold_in(seeds[7], 71), 0),
        "m_count": draw_m_count(jax.random.fold_in(seeds[7], 71), 0),
    }


HIGH = lax.Precision.HIGHEST

def gram(left, right):
    return jnp.einsum('bkc,blc->kl', left, right, precision=HIGH)

def times_small(vectors, small):
    return jnp.einsum('bkc,kl->blc', vectors, small, precision=HIGH)

def normalize(vectors, total_rows):
    lower_factor = jnp.linalg.cholesky(gram(vectors, vectors) / total_rows)
    identity = jnp.eye(vectors.shape[1], dtype=jnp.float32)
    inverse = jax.scipy.linalg.solve_triangular(lower_factor, identity, lower=True)
    return jnp.einsum('kl,blc->bkc', inverse, vectors, precision=HIGH)

def apply_a(a_tiles, a_cols, vector):
    vector = lax.optimization_barrier(vector)
    devices_count = NB // BR_DEV

    def one_block(pieces):
        tile_set, col_ids = pieces
        picked = vector[col_ids].astype(jnp.float32)
        return jnp.einsum('bjrc,bjic->bri', picked, tile_set.astype(jnp.float32))
    blocks = lax.map(one_block, (a_tiles.reshape(devices_count, BR_DEV, KA, TILE, TILE), a_cols.reshape(devices_count, BR_DEV, KA)))
    return blocks.reshape(NB, NRHS, TILE)

def apply_a_t(a_tiles, a_cols, vector):
    vector = lax.optimization_barrier(vector)
    devices_count = NB // BR_DEV

    def add_block(summed, pieces):
        tile_set, col_ids, part_vec = pieces
        contrib = jnp.einsum('bri,bjic->bjrc', part_vec.astype(jnp.float32), tile_set.astype(jnp.float32))
        return (summed.at[col_ids.reshape(-1)].add(contrib.reshape(-1, NRHS, TILE)), None)
    summed, ignored = lax.scan(add_block, jnp.zeros((NB, NRHS, TILE), jnp.float32), (a_tiles.reshape(devices_count, BR_DEV, KA, TILE, TILE), a_cols.reshape(devices_count, BR_DEV, KA), vector.reshape(devices_count, BR_DEV, NRHS, TILE)))
    return summed

def apply_m(m_tiles, m_rows, m_cols, m_count, vector):
    vector = lax.optimization_barrier(vector)
    devices_count = NB // BR_DEV

    def one_device(pieces):
        tile_set, row_ids, col_ids, live_count, device = pieces
        live_mask = (jnp.arange(TILE_DEV, dtype=jnp.int32) < live_count).astype(jnp.float32)
        picked = vector[col_ids].astype(jnp.float32)
        contrib = jnp.einsum('nrc,nic->nri', picked, tile_set.astype(jnp.float32)) * live_mask[:, None, None]
        local_rows = row_ids - device * BR_DEV
        return jax.ops.segment_sum(contrib, local_rows, num_segments=BR_DEV)
    blocks = lax.map(one_device, (m_tiles.reshape(devices_count, TILE_DEV, TILE, TILE), m_rows.reshape(devices_count, TILE_DEV), m_cols.reshape(devices_count, TILE_DEV), m_count, jnp.arange(devices_count, dtype=jnp.int32)))
    return blocks.reshape(NB, NRHS, TILE)

def apply_m_t(m_tiles, m_rows, m_cols, m_count, vector):
    vector = lax.optimization_barrier(vector)
    devices_count = NB // BR_DEV

    def add_device(summed, pieces):
        tile_set, row_ids, col_ids, live_count = pieces
        live_mask = (jnp.arange(TILE_DEV, dtype=jnp.int32) < live_count).astype(jnp.float32)
        picked = vector[row_ids].astype(jnp.float32)
        contrib = jnp.einsum('nri,nic->nrc', picked, tile_set.astype(jnp.float32)) * live_mask[:, None, None]
        return (summed.at[col_ids].add(contrib), None)
    summed, ignored = lax.scan(add_device, jnp.zeros((NB, NRHS, TILE), jnp.float32), (m_tiles.reshape(devices_count, TILE_DEV, TILE, TILE), m_rows.reshape(devices_count, TILE_DEV), m_cols.reshape(devices_count, TILE_DEV), m_count))
    return summed

def reference(right_side, a_tiles, a_cols, m_tiles, m_rows, m_cols, m_count):
    total_rows = NB * TILE
    basis = normalize(right_side, total_rows)
    shadow = basis
    solution = jnp.zeros_like(right_side)
    residual = right_side
    for iteration in range(ITERS):
        precond = apply_m(m_tiles, m_rows, m_cols, m_count, basis.astype(jnp.bfloat16))
        image = apply_a(a_tiles, a_cols, precond.astype(jnp.bfloat16))
        back = apply_a_t(a_tiles, a_cols, shadow.astype(jnp.bfloat16))
        back_image = apply_m_t(m_tiles, m_rows, m_cols, m_count, back.astype(jnp.bfloat16))
        coupling = gram(shadow, image) / total_rows
        factor = jnp.linalg.cholesky(gram(image, image))
        weights = jax.scipy.linalg.cho_solve((factor, True), gram(image, residual))
        solution = solution + times_small(precond, weights)
        residual = residual - times_small(image, weights)
        next_basis = image - times_small(basis, coupling)
        next_shadow = back_image - times_small(shadow, coupling.T)
        basis = normalize(next_basis, total_rows)
        shadow = normalize(next_shadow, total_rows)
    return (solution, residual, basis, shadow)
```

```python
import functools

import jax
import jax.numpy as jnp
from jax import lax
from jax.experimental import pallas as pl
from jax.experimental.pallas import tpu as pltpu
from jax.sharding import PartitionSpec as P

ITERS = 2
REACH_A = 16
REACH_M = 32
AXES = ("dom", "bal")
MESH = pl.DeviceIdType.MESH
F32 = jnp.float32
BF16 = jnp.bfloat16
VMEM_BYTES = 48 * 1024 * 1024

NN = (((1,), (0,)), ((), ()))
NT = (((1,), (1,)), ((), ()))


def low_dot(a, b, dims):
    return lax.dot_general(a, b, dims, preferred_element_type=F32)


def split(x):
    hi = x.astype(BF16)
    return hi, (x - hi.astype(F32)).astype(BF16)


def dot3(a, b, dims=NN):
    ah, al = split(a)
    bh, bl = split(b)
    return low_dot(ah, bh, dims) + (low_dot(ah, bl, dims) + low_dot(al, bh, dims))


def wide(ref):
    return jnp.concatenate([ref[b] for b in range(ref.shape[0])], axis=1)


def put_wide(ref, value):
    width = ref.shape[2]
    for b in range(ref.shape[0]):
        ref[b] = value[:, b * width : (b + 1) * width].astype(ref.dtype)


def beside(left, right):
    return jnp.concatenate([left, right], axis=0)


def right_half(x):
    half = x.shape[1] // 2
    return pltpu.roll(x, half, 1)[:, :half]


def inverse_factors(mats):
    size, lanes = mats[0].shape
    row = lax.broadcasted_iota(jnp.int32, (size, lanes), 0)
    lane = lax.broadcasted_iota(jnp.int32, (size, lanes), 1)
    unit = jnp.where(lane - size == row, 1.0, 0.0).astype(F32)
    state = []
    for m in mats:
        full = jnp.where(lane < size, m, unit)
        state.append([full[b * 8 : b * 8 + 8] for b in range(size // 8)])
    sub = lax.broadcasted_iota(jnp.int32, (8, lanes), 0)
    pivots = [[jnp.ones((8, lanes), F32) for _ in range(size // 8)] for _ in mats]
    for k in range(size):
        first, s = k // 8, k % 8
        for i, blocks in enumerate(state):
            pivot_row = blocks[first][s : s + 1, :]
            d = pivot_row[:, k : k + 1]
            scaled = jnp.broadcast_to(pivot_row * (1.0 / d), (8, lanes))
            pivots[i][first] = jnp.where(
                sub == s, jnp.broadcast_to(d, (8, lanes)), pivots[i][first]
            )
            for b in range(first, size // 8):
                column = jnp.broadcast_to(blocks[b][:, k : k + 1], (8, lanes))
                if b == first:
                    column = jnp.where(sub > s, column, 0.0)
                blocks[b] = blocks[b] - column * scaled
    out = []
    for blocks, piv in zip(state, pivots):
        full = jnp.concatenate([blk * lax.rsqrt(p) for blk, p in zip(blocks, piv)], axis=0)
        out.append(right_half(full))
    return out


def scatter_a(cols, vec_ref, a_ref, ext, ext_low, own, reach):
    rows, slots = a_ref.shape[0], a_ref.shape[1]
    ext[...] = jnp.zeros_like(ext)
    for r in range(rows):
        y = vec_ref[r]
        for j in range(slots):
            c = cols[r * slots + j]
            ext[c] = ext[c] + low_dot(y, a_ref[r, j], NN)
    ext_low[...] = ext[...].astype(BF16)
    own[...] = ext[reach : reach + rows]


def me_index(nb):
    return lax.axis_index("dom") * nb + lax.axis_index("bal")


def place(t, nb):
    return (lax.div(t, nb), lax.rem(t, nb))


def strides(span):
    return [s for k in range(1, span + 1) for s in (k, -k)]


def in_range(t, n):
    return jnp.logical_and(t >= 0, t < n)


def neighbour_greet(barrier, me, n, nb, span):
    total = 0
    for s in strides(span):
        ok = in_range(me + s, n)

        @pl.when(ok)
        def _(s=s):
            pl.semaphore_signal(barrier, inc=1, device_id=place(me + s, nb), device_id_type=MESH)

        total = total + ok.astype(jnp.int32)
    return total


def window_copies(src, window, send, recv, me, nb, span, rows):
    out = []
    for i, s in enumerate(strides(span)):
        out.append(
            (
                s,
                pltpu.make_async_remote_copy(
                    src_ref=src,
                    dst_ref=window.at[pl.ds((span - s) * rows, rows)],
                    send_sem=send.at[i],
                    recv_sem=recv.at[i],
                    device_id=place(me + s, nb),
                    device_id_type=MESH,
                ),
            )
        )
    return out


def give_copies(ext, landing, send, recv, me, nb, span, rows):
    out = []
    for i, s in enumerate(strides(span)):
        out.append(
            (
                s,
                pltpu.make_async_remote_copy(
                    src_ref=ext.at[pl.ds((span + s) * rows, rows)],
                    dst_ref=landing.at[i],
                    send_sem=send.at[i],
                    recv_sem=recv.at[i],
                    device_id=place(me + s, nb),
                    device_id_type=MESH,
                ),
            )
        )
    return out


def start_all(copies, me, n):
    for s, copy in copies:

        @pl.when(in_range(me + s, n))
        def _(copy=copy):
            copy.start()


def wait_sent(copies, me, n):
    for s, copy in copies:

        @pl.when(in_range(me + s, n))
        def _(copy=copy):
            copy.wait_send()


def wait_window(copies, window, me, n, span, rows):
    for s, copy in copies:
        ok = in_range(me - s, n)

        @pl.when(ok)
        def _(copy=copy):
            copy.wait_recv()

        @pl.when(jnp.logical_not(ok))
        def _(s=s):
            at = (span - s) * rows
            window[at : at + rows] = jnp.zeros((rows,) + tuple(window.shape[1:]), window.dtype)


def wait_given(copies, landing, total, me, n):
    for i, (s, copy) in enumerate(copies):

        @pl.when(in_range(me - s, n))
        def _(i=i, copy=copy):
            copy.wait_recv()
            total[...] = total[...] + landing[i].astype(F32)


def group_greet(barrier, dom, nb):
    d, b = lax.axis_index("dom"), lax.axis_index("bal")
    for o in range(1, nb):
        pl.semaphore_signal(
            barrier, inc=1, device_id=(d, lax.rem(b + o, nb)), device_id_type=MESH
        )
    for o in range(1, dom):
        pl.semaphore_signal(
            barrier, inc=1, device_id=(lax.rem(d + o, dom), b), device_id_type=MESH
        )
    return nb - 1 + dom - 1


def group_copies(src, slots, send, recv, dom, nb, axis):
    d, b = lax.axis_index("dom"), lax.axis_index("bal")
    size = dom if axis == "dom" else nb
    out = []
    for o in range(1, size):
        target = (lax.rem(d + o, dom), b) if axis == "dom" else (d, lax.rem(b + o, nb))
        out.append(
            pltpu.make_async_remote_copy(
                src_ref=src,
                dst_ref=slots.at[o - 1],
                send_sem=send.at[o - 1],
                recv_sem=recv.at[o - 1],
                device_id=target,
                device_id_type=MESH,
            )
        )
    return out


class Reduce:
    def __init__(self, part, slots_b, slots_d, send_b, recv_b, send_d, recv_d, dom, nb):
        self.part, self.slots_b, self.slots_d = part, slots_b, slots_d
        self.first = group_copies(part.at[0], slots_b, send_b, recv_b, dom, nb, "bal")
        self.second = group_copies(part.at[1], slots_d, send_d, recv_d, dom, nb, "dom")

    def start(self, value):
        self.part[0] = value
        for copy in self.first:
            copy.start()

    def finish(self):
        total = self.part[0]
        for o, copy in enumerate(self.first):
            copy.wait_recv()
            total = total + self.slots_b[o]
        self.part[1] = total
        for copy in self.second:
            copy.start()
        for o, copy in enumerate(self.second):
            copy.wait_recv()
            total = total + self.slots_d[o]
        for copy in self.first + self.second:
            copy.wait_send()
        return total


def reduce_scratch(height, lanes, dom, nb):
    dma = pltpu.SemaphoreType.DMA
    return [
        pltpu.VMEM((2, height, lanes), F32),
        pltpu.VMEM((nb - 1, height, lanes), F32),
        pltpu.VMEM((dom - 1, height, lanes), F32),
        dma((nb - 1,)),
        dma((nb - 1,)),
        dma((dom - 1,)),
        dma((dom - 1,)),
    ]


def start_gram_kernel(dom, nb, x_ref, out_ref, *red):
    barrier = pltpu.get_barrier_semaphore()
    pl.semaphore_wait(barrier, group_greet(barrier, dom, nb))
    reduce = Reduce(*red, dom, nb)
    x = wide(x_ref)
    reduce.start(dot3(x, beside(x, jnp.zeros_like(x)), NT))
    out_ref[...] = reduce.finish()


def start_basis_kernel(
    total_rows, cols, gram_ref, x_ref, a_ref, basis, basis_low, ext_low, own, ext
):
    (inverse,) = inverse_factors([gram_ref[...] * (1.0 / total_rows)])
    value = dot3(inverse, wide(x_ref))
    put_wide(basis, value)
    put_wide(basis_low, value)
    scatter_a(cols, basis_low, a_ref, ext, ext_low, own, REACH_A)


def first_exchange_kernel(
    n, nb, basis_low, ext_low, own, window, back_low, landing, total, ws, wr, gs, gr
):
    rows = basis_low.shape[0]
    span_m, span_a = REACH_M // rows, REACH_A // rows
    me = me_index(nb)
    barrier = pltpu.get_barrier_semaphore()
    pl.semaphore_wait(barrier, neighbour_greet(barrier, me, n, nb, max(span_m, span_a)))
    gives = give_copies(ext_low, landing, gs, gr, me, nb, span_a, rows)
    copies = window_copies(basis_low, window, ws, wr, me, nb, span_m, rows)
    start_all(gives, me, n)
    start_all(copies, me, n)
    at = span_m * rows
    window[at : at + rows] = basis_low[...]
    total[...] = own[...]
    wait_given(gives, landing, total, me, n)
    back_low[...] = total[...].astype(BF16)
    wait_window(copies, window, me, n, span_m, rows)
    wait_sent(gives, me, n)
    wait_sent(copies, me, n)


def inverse_apply_kernel(
    group, row_ref, col_ref, count_ref, window, back_low, tiles, precond, precond_low, ext_low, own, ext
):
    rows = precond.shape[0]
    count = count_ref[0]
    precond[...] = jnp.zeros_like(precond)
    ext[...] = jnp.zeros_like(ext)

    def step(g, carry):
        for u in range(group):
            s = g * group + u
            r, c = row_ref[s], col_ref[s]
            live = s < count
            tile = tiles[s]
            ahead = low_dot(window[c], tile, NT)
            behind = low_dot(back_low[r], tile, NN)
            precond[r] = precond[r] + jnp.where(live, ahead, 0.0)
            ext[c] = ext[c] + jnp.where(live, behind, 0.0)
        return carry

    lax.fori_loop(0, lax.div(count + group - 1, group), step, 0)
    precond_low[...] = precond[...].astype(BF16)
    ext_low[...] = ext[...].astype(BF16)
    own[...] = ext[REACH_M : REACH_M + rows]


def second_exchange_kernel(
    n,
    dom,
    nb,
    total_rows,
    cols,
    precond_low,
    ext_low,
    own,
    a_ref,
    basis_ref,
    shadow_ref,
    residual_ref,
    image_out,
    u_out,
    s_out,
    mats1,
    mats2,
    window,
    landing,
    total,
    ws,
    wr,
    gs,
    gr,
    *red,
):
    rows, slots = a_ref.shape[0], a_ref.shape[1]
    span_m, span_a = REACH_M // rows, REACH_A // rows
    me = me_index(nb)
    barrier = pltpu.get_barrier_semaphore()
    greeted = neighbour_greet(barrier, me, n, nb, max(span_m, span_a))
    pl.semaphore_wait(barrier, greeted + group_greet(barrier, dom, nb))
    copies = window_copies(precond_low, window, ws, wr, me, nb, span_a, rows)
    gives = give_copies(ext_low, landing, gs, gr, me, nb, span_m, rows)
    start_all(copies, me, n)
    start_all(gives, me, n)
    at = span_a * rows
    window[at : at + rows] = precond_low[...]
    total[...] = own[...]
    wait_window(copies, window, me, n, span_a, rows)
    for r in range(rows):
        value = low_dot(window[cols[r * slots]], a_ref[r, 0], NT)
        for j in range(1, slots):
            value = value + low_dot(window[cols[r * slots + j]], a_ref[r, j], NT)
        image_out[r] = value
    image, shadow, residual = wide(image_out), wide(shadow_ref), wide(residual_ref)
    none = jnp.zeros_like(image)
    first = Reduce(*red[:7], dom, nb)
    image_left, image_right = beside(image, none), beside(none, image)
    first.start(
        beside(
            dot3(image, image_left, NT) + dot3(residual, image_right, NT),
            dot3(shadow, image_left, NT) + dot3(image, beside(none, shadow), NT),
        )
    )
    wait_given(gives, landing, total, me, n)
    sums = first.finish()
    mats1[...] = sums
    size = image.shape[0]
    both = sums[size:] * (1.0 / total_rows)
    coupling, coupling_t = both[:, :size], right_half(both)
    u = image - dot3(coupling_t, wide(basis_ref))
    s = wide(total) - dot3(coupling, shadow)
    put_wide(u_out, u)
    put_wide(s_out, s)
    second = Reduce(*red[7:], dom, nb)
    second.start(dot3(u, beside(u, none), NT) + dot3(s, beside(none, s), NT))
    mats2[...] = second.finish()
    wait_sent(copies, me, n)
    wait_sent(gives, me, n)


def update_kernel(is_first, is_last, total_rows, cols, *refs):
    refs = list(refs)
    mats1, mats2, image, u, s, precond, residual = refs[:7]
    refs = refs[7:]
    old = None if is_first else refs.pop(0)
    a_ref = None if is_last else refs.pop(0)
    solution_out, residual_out, basis, shadow = refs[:4]
    size = image.shape[1]
    grams = mats2[...] * (1.0 / total_rows)
    normal = mats1[:size, :]
    inv_u, inv_s, inv_n = inverse_factors([grams, pltpu.roll(grams, size, 1), normal])
    weights_t = dot3(dot3(right_half(normal), inv_n, NT), inv_n)
    new_basis = dot3(inv_u, wide(u))
    put_wide(basis, new_basis)
    put_wide(shadow, dot3(inv_s, wide(s)))
    gained = dot3(weights_t, wide(precond))
    put_wide(solution_out, gained if is_first else wide(old) + gained)
    put_wide(residual_out, wide(residual) - dot3(weights_t, wide(image)))
    if not is_last:
        basis_low, ext_low, own, ext, shadow_low = refs[4:]
        put_wide(basis_low, new_basis)
        shadow_low[...] = shadow[...].astype(BF16)
        scatter_a(cols, shadow_low, a_ref, ext, ext_low, own, REACH_A)


def call(kernel, outs, args, scalars, scratch=(), collective=None):
    params = dict(vmem_limit_bytes=VMEM_BYTES)
    if collective is not None:
        params.update(collective_id=collective, has_side_effects=True)
    specs = [pl.BlockSpec(memory_space=pltpu.SMEM)] * scalars
    specs += [pl.BlockSpec(memory_space=pltpu.VMEM)] * (len(args) - scalars)
    return pl.pallas_call(
        kernel,
        out_shape=outs,
        in_specs=specs,
        out_specs=[pl.BlockSpec(memory_space=pltpu.VMEM)] * len(outs),
        scratch_shapes=list(scratch),
        compiler_params=pltpu.CompilerParams(**params),
    )(*args)


def shards(right_side, a_tiles, a_cols, m_tiles, m_rows, m_cols, m_count):
    rows, size, width = right_side.shape
    dom, nb = lax.axis_size("dom"), lax.axis_size("bal")
    n = dom * nb
    total_rows = rows * width * n
    span_a, span_m = REACH_A // rows, REACH_M // rows
    first_row = lax.axis_index(AXES) * rows
    a_win = (a_cols - first_row + REACH_A).reshape(-1)
    row_local = m_rows - first_row
    m_win = m_cols - first_row + REACH_M
    group = max(g for g in (8, 4, 2, 1) if m_tiles.shape[0] % g == 0)

    def shape(dtype, count=rows):
        return jax.ShapeDtypeStruct((count, size, width), dtype)

    high, low = shape(F32), shape(BF16)
    ext_a, ext_m = rows + 2 * REACH_A, rows + 2 * REACH_M
    dma = pltpu.SemaphoreType.DMA

    def landing(span):
        return pltpu.VMEM((2 * span, rows, size, width), BF16)

    def sems(*spans):
        return [dma((2 * sp,)) for sp in spans for _ in range(2)]

    (start,) = call(
        functools.partial(start_gram_kernel, dom, nb),
        [jax.ShapeDtypeStruct((size, 2 * size), F32)],
        [right_side],
        0,
        reduce_scratch(size, 2 * size, dom, nb),
        0,
    )
    basis, basis_low, given_a, own_a = call(
        functools.partial(start_basis_kernel, total_rows),
        [high, low, shape(BF16, ext_a), high],
        [a_win, start, right_side, a_tiles],
        1,
        [pltpu.VMEM((ext_a, size, width), F32)],
    )
    shadow, residual, solved = basis, right_side, None
    for iteration in range(ITERS):
        is_first, is_last = iteration == 0, iteration == ITERS - 1
        window, back_low = call(
            functools.partial(first_exchange_kernel, n, nb),
            [shape(BF16, ext_m), low],
            [basis_low, given_a, own_a],
            0,
            [landing(span_a), pltpu.VMEM((rows, size, width), F32)] + sems(span_m, span_a),
            1,
        )
        precond, precond_low, given_m, own_m = call(
            functools.partial(inverse_apply_kernel, group),
            [high, low, shape(BF16, ext_m), high],
            [row_local, m_win, m_count, window, back_low, m_tiles],
            3,
            [pltpu.VMEM((ext_m, size, width), F32)],
        )
        image, u, s, mats1, mats2 = call(
            functools.partial(second_exchange_kernel, n, dom, nb, total_rows),
            [high] * 3
            + [
                jax.ShapeDtypeStruct((2 * size, 2 * size), F32),
                jax.ShapeDtypeStruct((size, 2 * size), F32),
            ],
            [a_win, precond_low, given_m, own_m, a_tiles, basis, shadow, residual],
            1,
            [
                pltpu.VMEM((ext_a, size, width), BF16),
                landing(span_m),
                pltpu.VMEM((rows, size, width), F32),
            ]
            + sems(span_a, span_m)
            + reduce_scratch(2 * size, 2 * size, dom, nb)
            + reduce_scratch(size, 2 * size, dom, nb),
            2,
        )
        args = [a_win, mats1, mats2, image, u, s, precond, residual]
        outs, scratch = [high] * 4, []
        if not is_first:
            args.append(solved)
        if not is_last:
            args.append(a_tiles)
            outs = outs + [low, shape(BF16, ext_a), high]
            scratch = [pltpu.VMEM((ext_a, size, width), F32), pltpu.VMEM((rows, size, width), BF16)]
        results = call(
            functools.partial(update_kernel, is_first, is_last, total_rows), outs, args, 1, scratch
        )
        solved, residual, basis, shadow = results[:4]
        if not is_last:
            basis_low, given_a, own_a = results[4:]
    return (solved, residual, basis, shadow)


def solution(mesh):
    vector = P(AXES, None, None)
    placed = (
        vector,
        P(AXES, None, None, None),
        P(AXES, None),
        P(AXES, None, None),
        P(AXES),
        P(AXES),
        P(AXES),
    )
    return jax.shard_map(
        shards, mesh=mesh, in_specs=placed, out_specs=(vector,) * 4, check_vma=False
    )
```

```python
import functools

import jax
import jax.numpy as jnp
from jax import lax
from jax.experimental import pallas as pl
from jax.experimental.pallas import tpu as pltpu
from jax.sharding import PartitionSpec as P

ITERS = 2
REACH_A = 16
REACH_M = 32
AXES = ("dom", "bal")
MESH = pl.DeviceIdType.MESH
F32 = jnp.float32
BF16 = jnp.bfloat16
VMEM_BYTES = 48 * 1024 * 1024

NN = (((1,), (0,)), ((), ()))
NT = (((1,), (1,)), ((), ()))


def low_dot(a, b, dims):
    return lax.dot_general(a, b, dims, preferred_element_type=F32)


def split(x):
    hi = x.astype(BF16)
    return hi, (x - hi.astype(F32)).astype(BF16)


def dot3(a, b, dims=NN):
    ah, al = split(a)
    bh, bl = split(b)
    return low_dot(ah, bh, dims) + (low_dot(ah, bl, dims) + low_dot(al, bh, dims))


def wide(ref):
    return jnp.concatenate([ref[b] for b in range(ref.shape[0])], axis=1)


def put_wide(ref, value):
    width = ref.shape[2]
    for b in range(ref.shape[0]):
        ref[b] = value[:, b * width : (b + 1) * width].astype(ref.dtype)


def beside(left, right):
    return jnp.concatenate([left, right], axis=0)


def right_half(x):
    half = x.shape[1] // 2
    return pltpu.roll(x, half, 1)[:, :half]


def inverse_factors(mats):
    size, lanes = mats[0].shape
    row = lax.broadcasted_iota(jnp.int32, (size, lanes), 0)
    lane = lax.broadcasted_iota(jnp.int32, (size, lanes), 1)
    unit = jnp.where(lane - size == row, 1.0, 0.0).astype(F32)
    state = []
    for m in mats:
        full = jnp.where(lane < size, m, unit)
        state.append([full[b * 8 : b * 8 + 8] for b in range(size // 8)])
    sub = lax.broadcasted_iota(jnp.int32, (8, lanes), 0)
    pivots = [[jnp.ones((8, lanes), F32) for _ in range(size // 8)] for _ in mats]
    for k in range(size):
        first, s = k // 8, k % 8
        for i, blocks in enumerate(state):
            pivot_row = blocks[first][s : s + 1, :]
            d = pivot_row[:, k : k + 1]
            scaled = jnp.broadcast_to(pivot_row * (1.0 / d), (8, lanes))
            pivots[i][first] = jnp.where(
                sub == s, jnp.broadcast_to(d, (8, lanes)), pivots[i][first]
            )
            for b in range(first, size // 8):
                column = jnp.broadcast_to(blocks[b][:, k : k + 1], (8, lanes))
                if b == first:
                    column = jnp.where(sub > s, column, 0.0)
                blocks[b] = blocks[b] - column * scaled
    out = []
    for blocks, piv in zip(state, pivots):
        full = jnp.concatenate([blk * lax.rsqrt(p) for blk, p in zip(blocks, piv)], axis=0)
        out.append(right_half(full))
    return out


def scatter_a(cols, vec_ref, a_ref, ext, ext_low, own, reach):
    rows, slots = a_ref.shape[0], a_ref.shape[1]
    ext[...] = jnp.zeros_like(ext)
    for r in range(rows):
        y = vec_ref[r]
        for j in range(slots):
            c = cols[r * slots + j]
            ext[c] = ext[c] + low_dot(y, a_ref[r, j], NN)
    ext_low[...] = ext[...].astype(BF16)
    own[...] = ext[reach : reach + rows]


def me_index(nb):
    return lax.axis_index("dom") * nb + lax.axis_index("bal")


def place(t, nb):
    return (lax.div(t, nb), lax.rem(t, nb))


def strides(span):
    return [s for k in range(2, span + 1, 2) for s in (k, -k)]


def in_range(t, n):
    return jnp.logical_and(t >= 0, t < n)


def reaches(t, distance, span, n):
    return jnp.logical_and(in_range(t, n), jnp.abs(distance) <= span)


def toward_partner(me):
    return 1 - 2 * lax.rem(me, 2)


def neighbour_greet(barrier, me, n, nb, span):
    total = 1
    pl.semaphore_signal(
        barrier, inc=1, device_id=place(me + toward_partner(me), nb), device_id_type=MESH
    )
    for s in strides(span):
        ok = in_range(me + s, n)

        @pl.when(ok)
        def _(s=s):
            pl.semaphore_signal(barrier, inc=1, device_id=place(me + s, nb), device_id_type=MESH)

        total = total + ok.astype(jnp.int32)
    return total


def remote(src, dst, send, recv, target, nb):
    return pltpu.make_async_remote_copy(
        src_ref=src,
        dst_ref=dst,
        send_sem=send,
        recv_sem=recv,
        device_id=place(target, nb),
        device_id_type=MESH,
    )


class Window:
    def __init__(self, src, window, send, recv, psend, precv, me, n, nb, span):
        rows = src.shape[0]
        self.src, self.window, self.rows, self.span, self.me, self.n = src, window, rows, span, me, n
        go = toward_partner(me)
        partner = me + go
        self.own = remote(
            src, window.at[pl.ds((span - go) * rows, rows)], psend.at[span], precv.at[span], partner, nb
        )
        self.direct, self.relays = [], []
        for i, s in enumerate(strides(span)):
            here = window.at[pl.ds((span - s) * rows, rows)]
            copy = remote(src, here, send.at[i], recv.at[i], me + s, nb)
            self.direct.append((in_range(me + s, n), in_range(me - s, n), copy))
            give = reaches(me - s, s + go, span, n)
            get = reaches(partner - s, s - go, span, n)
            at = jnp.clip(span - s - go, 0, 2 * span) * rows
            relay = remote(
                here, window.at[pl.ds(at, rows)], psend.at[i], precv.at[i], partner, nb
            )
            self.relays.append((give, get, relay))

    def start(self):
        for ok, _, copy in self.direct:
            pl.when(ok)(copy.start)
        self.own.start()
        at = self.span * self.rows
        self.window[at : at + self.rows] = self.src[...]
        for s in range(-self.span, self.span + 1):
            if s != 0:

                @pl.when(jnp.logical_not(in_range(self.me - s, self.n)))
                def _(s=s):
                    at = (self.span - s) * self.rows
                    self.window[at : at + self.rows] = jnp.zeros(self.src.shape, self.window.dtype)

    def relay(self):
        for (_, arrives, copy), (give, _, relay) in zip(self.direct, self.relays):
            pl.when(arrives)(copy.wait_recv)
            pl.when(give)(relay.start)

    def finish(self):
        self.own.wait_recv()
        for _, get, relay in self.relays:
            pl.when(get)(relay.wait_recv)

    def sent(self):
        self.own.wait_send()
        for (ok, _, copy), (give, _, relay) in zip(self.direct, self.relays):
            pl.when(ok)(copy.wait_send)
            pl.when(give)(relay.wait_send)


class GiveBack:
    def __init__(self, ext, near, outgoing, landing, send, recv, psend, precv, me, n, nb, span, rows):
        self.ext, self.near, self.outgoing, self.landing = ext, near, outgoing, landing
        self.rows, self.span = rows, span
        go = toward_partner(me)
        partner = me + go
        self.own = remote(
            ext.at[pl.ds((span + go) * rows, rows)],
            near.at[span],
            psend.at[span],
            precv.at[span],
            partner,
            nb,
        )
        self.swaps, self.direct = [], []
        for i, s in enumerate(strides(span)):
            give = reaches(partner + s, s + go, span, n)
            get = reaches(me + s, s - go, span, n)
            at = jnp.clip(span + s + go, 0, 2 * span) * rows
            swap = remote(ext.at[pl.ds(at, rows)], near.at[i], psend.at[i], precv.at[i], partner, nb)
            self.swaps.append((give, get, swap))
            copy = remote(outgoing.at[i], landing.at[i], send.at[i], recv.at[i], me + s, nb)
            self.direct.append((in_range(me + s, n), in_range(me - s, n), copy))

    def start(self):
        for give, _, swap in self.swaps:
            pl.when(give)(swap.start)
        self.own.start()

    def forward(self):
        for i, s in enumerate(strides(self.span)):
            give, get, swap = self.swaps[i]
            ok, _, copy = self.direct[i]
            at = (self.span + s) * self.rows

            @pl.when(get)
            def _(i=i, at=at, swap=swap):
                swap.wait_recv()
                both = self.ext[at : at + self.rows].astype(F32) + self.near[i].astype(F32)
                self.outgoing[i] = both.astype(BF16)

            @pl.when(jnp.logical_not(get))
            def _(i=i, at=at):
                self.outgoing[i] = self.ext[at : at + self.rows]

            pl.when(ok)(copy.start)

    def finish(self, total):
        self.own.wait_recv()
        total[...] = total[...] + self.near[self.span].astype(F32)
        for i, (_, arrives, copy) in enumerate(self.direct):

            @pl.when(arrives)
            def _(i=i, copy=copy):
                copy.wait_recv()
                total[...] = total[...] + self.landing[i].astype(F32)

    def sent(self):
        self.own.wait_send()
        for (give, _, swap), (ok, _, copy) in zip(self.swaps, self.direct):
            pl.when(give)(swap.wait_send)
            pl.when(ok)(copy.wait_send)


def group_greet(barrier, dom, nb):
    d, b = lax.axis_index("dom"), lax.axis_index("bal")
    for o in range(1, nb):
        pl.semaphore_signal(
            barrier, inc=1, device_id=(d, lax.rem(b + o, nb)), device_id_type=MESH
        )
    for o in range(1, dom):
        pl.semaphore_signal(
            barrier, inc=1, device_id=(lax.rem(d + o, dom), b), device_id_type=MESH
        )
    return nb - 1 + dom - 1


def group_targets(dom, nb, axis):
    d, b = lax.axis_index("dom"), lax.axis_index("bal")
    if axis == "dom":
        return [(lax.rem(d + o, dom), b) for o in range(1, dom)]
    return [(d, lax.rem(b + o, nb)) for o in range(1, nb)]


class Reduce:
    def __init__(self, part, slots_b, mid, slots_d, whole, s1, r1, s2, r2, s3, r3, dom, nb):
        self.part, self.slots_b, self.mid, self.slots_d, self.whole = part, slots_b, mid, slots_d, whole
        self.place = lax.axis_index("bal")
        bal, far = group_targets(dom, nb, "bal"), group_targets(dom, nb, "dom")

        def copies(source, dest, targets, send, recv):
            return [
                pltpu.make_async_remote_copy(
                    src_ref=source(t),
                    dst_ref=dest(o),
                    send_sem=send.at[o],
                    recv_sem=recv.at[o],
                    device_id=t,
                    device_id_type=MESH,
                )
                for o, t in enumerate(targets)
            ]

        mine = whole.at[self.place]
        self.scatter = copies(lambda t: part.at[t[1]], lambda o: slots_b.at[o], bal, s1, r1)
        self.across = copies(lambda t: mid, lambda o: slots_d.at[o], far, s2, r2)
        self.gather = copies(lambda t: mine, lambda o: mine, bal, s3, r3)

    def start(self, value):
        count, height = self.part.shape[0], self.part.shape[1]
        for i in range(count):
            self.part[i] = value[i * height : (i + 1) * height]
        for copy in self.scatter:
            copy.start()

    def finish(self):
        total = self.part[self.place]
        for o, copy in enumerate(self.scatter):
            copy.wait_recv()
            total = total + self.slots_b[o]
        self.mid[...] = total
        for copy in self.across:
            copy.start()
        for o, copy in enumerate(self.across):
            copy.wait_recv()
            total = total + self.slots_d[o]
        self.whole[self.place] = total
        for copy in self.gather:
            copy.start()
        for copy in self.gather:
            copy.wait_recv()
        for copy in self.scatter + self.across + self.gather:
            copy.wait_send()
        return jnp.concatenate([self.whole[i] for i in range(self.whole.shape[0])], axis=0)


def reduce_scratch(height, lanes, dom, nb):
    dma = pltpu.SemaphoreType.DMA
    piece = height // nb
    return [
        pltpu.VMEM((nb, piece, lanes), F32),
        pltpu.VMEM((nb - 1, piece, lanes), F32),
        pltpu.VMEM((piece, lanes), F32),
        pltpu.VMEM((dom - 1, piece, lanes), F32),
        pltpu.VMEM((nb, piece, lanes), F32),
    ] + [dma((count - 1,)) for count in (nb, nb, dom, dom, nb, nb)]


def start_gram_kernel(dom, nb, x_ref, out_ref, *red):
    barrier = pltpu.get_barrier_semaphore()
    pl.semaphore_wait(barrier, group_greet(barrier, dom, nb))
    reduce = Reduce(*red, dom, nb)
    x = wide(x_ref)
    reduce.start(dot3(x, beside(x, jnp.zeros_like(x)), NT))
    out_ref[...] = reduce.finish()


def start_basis_kernel(
    total_rows, cols, gram_ref, x_ref, a_ref, basis, basis_low, ext_low, own, ext
):
    (inverse,) = inverse_factors([gram_ref[...] * (1.0 / total_rows)])
    value = dot3(inverse, wide(x_ref))
    put_wide(basis, value)
    put_wide(basis_low, value)
    scatter_a(cols, basis_low, a_ref, ext, ext_low, own, REACH_A)


def first_exchange_kernel(n, nb, basis_low, ext_low, own, window, back_low, total, *parts):
    rows = basis_low.shape[0]
    span_m, span_a = REACH_M // rows, REACH_A // rows
    me = me_index(nb)
    barrier = pltpu.get_barrier_semaphore()
    pl.semaphore_wait(barrier, neighbour_greet(barrier, me, n, nb, max(span_m, span_a)))
    fetch = Window(basis_low, window, *parts[:4], me, n, nb, span_m)
    give = GiveBack(ext_low, *parts[4:], me, n, nb, span_a, rows)
    give.start()
    fetch.start()
    give.forward()
    total[...] = own[...]
    fetch.relay()
    give.finish(total)
    back_low[...] = total[...].astype(BF16)
    fetch.finish()
    give.sent()
    fetch.sent()


def inverse_apply_kernel(
    group, row_ref, col_ref, count_ref, window, back_low, tiles, precond, precond_low, ext_low, own, ext
):
    rows = precond.shape[0]
    count = count_ref[0]
    precond[...] = jnp.zeros_like(precond)
    ext[...] = jnp.zeros_like(ext)

    def step(g, carry):
        for u in range(group):
            s = g * group + u
            r, c = row_ref[s], col_ref[s]
            live = s < count
            tile = tiles[s]
            ahead = low_dot(window[c], tile, NT)
            behind = low_dot(back_low[r], tile, NN)
            precond[r] = precond[r] + jnp.where(live, ahead, 0.0)
            ext[c] = ext[c] + jnp.where(live, behind, 0.0)
        return carry

    lax.fori_loop(0, lax.div(count + group - 1, group), step, 0)
    precond_low[...] = precond[...].astype(BF16)
    ext_low[...] = ext[...].astype(BF16)
    own[...] = ext[REACH_M : REACH_M + rows]


def second_exchange_kernel(
    n,
    dom,
    nb,
    total_rows,
    cols,
    precond_low,
    ext_low,
    own,
    a_ref,
    basis_ref,
    shadow_ref,
    residual_ref,
    image_out,
    u_out,
    s_out,
    mats1,
    mats2,
    window,
    total,
    *parts,
):
    rows, slots = a_ref.shape[0], a_ref.shape[1]
    span_m, span_a = REACH_M // rows, REACH_A // rows
    me = me_index(nb)
    barrier = pltpu.get_barrier_semaphore()
    greeted = neighbour_greet(barrier, me, n, nb, max(span_m, span_a))
    pl.semaphore_wait(barrier, greeted + group_greet(barrier, dom, nb))
    fetch = Window(precond_low, window, *parts[:4], me, n, nb, span_a)
    give = GiveBack(ext_low, *parts[4:11], me, n, nb, span_m, rows)
    red = parts[11:]
    fetch.start()
    give.start()
    fetch.relay()
    give.forward()
    total[...] = own[...]
    fetch.finish()
    for r in range(rows):
        value = low_dot(window[cols[r * slots]], a_ref[r, 0], NT)
        for j in range(1, slots):
            value = value + low_dot(window[cols[r * slots + j]], a_ref[r, j], NT)
        image_out[r] = value
    image, shadow, residual = wide(image_out), wide(shadow_ref), wide(residual_ref)
    none = jnp.zeros_like(image)
    first = Reduce(*red[:11], dom, nb)
    image_left, image_right = beside(image, none), beside(none, image)
    first.start(
        beside(
            dot3(image, image_left, NT) + dot3(residual, image_right, NT),
            dot3(shadow, image_left, NT) + dot3(image, beside(none, shadow), NT),
        )
    )
    give.finish(total)
    sums = first.finish()
    mats1[...] = sums
    size = image.shape[0]
    both = sums[size:] * (1.0 / total_rows)
    coupling, coupling_t = both[:, :size], right_half(both)
    u = image - dot3(coupling_t, wide(basis_ref))
    s = wide(total) - dot3(coupling, shadow)
    put_wide(u_out, u)
    put_wide(s_out, s)
    second = Reduce(*red[11:], dom, nb)
    second.start(dot3(u, beside(u, none), NT) + dot3(s, beside(none, s), NT))
    mats2[...] = second.finish()
    fetch.sent()
    give.sent()


def update_kernel(is_first, is_last, total_rows, cols, *refs):
    refs = list(refs)
    mats1, mats2, image, u, s, precond, residual = refs[:7]
    refs = refs[7:]
    old = None if is_first else refs.pop(0)
    a_ref = None if is_last else refs.pop(0)
    solution_out, residual_out, basis, shadow = refs[:4]
    size = image.shape[1]
    grams = mats2[...] * (1.0 / total_rows)
    normal = mats1[:size, :]
    inv_u, inv_s, inv_n = inverse_factors([grams, pltpu.roll(grams, size, 1), normal])
    weights_t = dot3(dot3(right_half(normal), inv_n, NT), inv_n)
    new_basis = dot3(inv_u, wide(u))
    put_wide(basis, new_basis)
    put_wide(shadow, dot3(inv_s, wide(s)))
    gained = dot3(weights_t, wide(precond))
    put_wide(solution_out, gained if is_first else wide(old) + gained)
    put_wide(residual_out, wide(residual) - dot3(weights_t, wide(image)))
    if not is_last:
        basis_low, ext_low, own, ext, shadow_low = refs[4:]
        put_wide(basis_low, new_basis)
        shadow_low[...] = shadow[...].astype(BF16)
        scatter_a(cols, shadow_low, a_ref, ext, ext_low, own, REACH_A)


def call(kernel, outs, args, scalars, scratch=(), collective=None):
    params = dict(vmem_limit_bytes=VMEM_BYTES)
    if collective is not None:
        params.update(collective_id=collective, has_side_effects=True)
    specs = [pl.BlockSpec(memory_space=pltpu.SMEM)] * scalars
    specs += [pl.BlockSpec(memory_space=pltpu.VMEM)] * (len(args) - scalars)
    return pl.pallas_call(
        kernel,
        out_shape=outs,
        in_specs=specs,
        out_specs=[pl.BlockSpec(memory_space=pltpu.VMEM)] * len(outs),
        scratch_shapes=list(scratch),
        compiler_params=pltpu.CompilerParams(**params),
    )(*args)


def shards(right_side, a_tiles, a_cols, m_tiles, m_rows, m_cols, m_count):
    rows, size, width = right_side.shape
    dom, nb = lax.axis_size("dom"), lax.axis_size("bal")
    n = dom * nb
    total_rows = rows * width * n
    span_a, span_m = REACH_A // rows, REACH_M // rows
    first_row = lax.axis_index(AXES) * rows
    a_win = (a_cols - first_row + REACH_A).reshape(-1)
    row_local = m_rows - first_row
    m_win = m_cols - first_row + REACH_M
    group = max(g for g in (8, 4, 2, 1) if m_tiles.shape[0] % g == 0)

    def shape(dtype, count=rows):
        return jax.ShapeDtypeStruct((count, size, width), dtype)

    high, low = shape(F32), shape(BF16)
    ext_a, ext_m = rows + 2 * REACH_A, rows + 2 * REACH_M
    dma = pltpu.SemaphoreType.DMA

    def sems(span):
        return [dma((span,)), dma((span,)), dma((span + 1,)), dma((span + 1,))]

    def give_scratch(span):
        return [
            pltpu.VMEM((count, rows, size, width), BF16) for count in (span + 1, span, span)
        ] + sems(span)

    (start,) = call(
        functools.partial(start_gram_kernel, dom, nb),
        [jax.ShapeDtypeStruct((size, 2 * size), F32)],
        [right_side],
        0,
        reduce_scratch(size, 2 * size, dom, nb),
        0,
    )
    basis, basis_low, given_a, own_a = call(
        functools.partial(start_basis_kernel, total_rows),
        [high, low, shape(BF16, ext_a), high],
        [a_win, start, right_side, a_tiles],
        1,
        [pltpu.VMEM((ext_a, size, width), F32)],
    )
    shadow, residual, solved = basis, right_side, None
    for iteration in range(ITERS):
        is_first, is_last = iteration == 0, iteration == ITERS - 1
        window, back_low = call(
            functools.partial(first_exchange_kernel, n, nb),
            [shape(BF16, ext_m), low],
            [basis_low, given_a, own_a],
            0,
            [pltpu.VMEM((rows, size, width), F32)] + sems(span_m) + give_scratch(span_a),
            1,
        )
        precond, precond_low, given_m, own_m = call(
            functools.partial(inverse_apply_kernel, group),
            [high, low, shape(BF16, ext_m), high],
            [row_local, m_win, m_count, window, back_low, m_tiles],
            3,
            [pltpu.VMEM((ext_m, size, width), F32)],
        )
        image, u, s, mats1, mats2 = call(
            functools.partial(second_exchange_kernel, n, dom, nb, total_rows),
            [high] * 3
            + [
                jax.ShapeDtypeStruct((2 * size, 2 * size), F32),
                jax.ShapeDtypeStruct((size, 2 * size), F32),
            ],
            [a_win, precond_low, given_m, own_m, a_tiles, basis, shadow, residual],
            1,
            [
                pltpu.VMEM((ext_a, size, width), BF16),
                pltpu.VMEM((rows, size, width), F32),
            ]
            + sems(span_a)
            + give_scratch(span_m)
            + reduce_scratch(2 * size, 2 * size, dom, nb)
            + reduce_scratch(size, 2 * size, dom, nb),
            2,
        )
        args = [a_win, mats1, mats2, image, u, s, precond, residual]
        outs, scratch = [high] * 4, []
        if not is_first:
            args.append(solved)
        if not is_last:
            args.append(a_tiles)
            outs = outs + [low, shape(BF16, ext_a), high]
            scratch = [pltpu.VMEM((ext_a, size, width), F32), pltpu.VMEM((rows, size, width), BF16)]
        results = call(
            functools.partial(update_kernel, is_first, is_last, total_rows), outs, args, 1, scratch
        )
        solved, residual, basis, shadow = results[:4]
        if not is_last:
            basis_low, given_a, own_a = results[4:]
    return (solved, residual, basis, shadow)


def solution(mesh):
    vector = P(AXES, None, None)
    placed = (
        vector,
        P(AXES, None, None, None),
        P(AXES, None),
        P(AXES, None, None),
        P(AXES),
        P(AXES),
        P(AXES),
    )
    return jax.shard_map(
        shards, mesh=mesh, in_specs=placed, out_specs=(vector,) * 4, check_vma=False
    )
```

```python
import functools

import jax
import jax.numpy as jnp
from jax import lax
from jax.experimental import pallas as pl
from jax.experimental.pallas import tpu as pltpu
from jax.sharding import PartitionSpec as P

ITERS = 2
REACH_A = 16
REACH_M = 32
AXES = ("dom", "bal")
MESH = pl.DeviceIdType.MESH
F32 = jnp.float32
BF16 = jnp.bfloat16
VMEM_BYTES = 16 * 1024 * 1024

NN = (((1,), (0,)), ((), ()))
NT = (((1,), (1,)), ((), ()))


def low_dot(a, b, dims):
    return lax.dot_general(a, b, dims, preferred_element_type=F32)


def split(x):
    hi = x.astype(BF16)
    return hi, (x - hi.astype(F32)).astype(BF16)


def dot3(a, b, dims=NN):
    ah, al = split(a)
    bh, bl = split(b)
    return low_dot(ah, bh, dims) + (low_dot(ah, bl, dims) + low_dot(al, bh, dims))


def wide(ref):
    return jnp.concatenate([ref[b] for b in range(ref.shape[0])], axis=1)


def put_wide(ref, value):
    width = ref.shape[2]
    for b in range(ref.shape[0]):
        ref[b] = value[:, b * width : (b + 1) * width].astype(ref.dtype)


def beside(left, right):
    return jnp.concatenate([left, right], axis=0)


def right_half(x):
    half = x.shape[1] // 2
    return pltpu.roll(x, half, 1)[:, :half]


def inverse_factors(mats):
    size, lanes = mats[0].shape
    row = lax.broadcasted_iota(jnp.int32, (size, lanes), 0)
    lane = lax.broadcasted_iota(jnp.int32, (size, lanes), 1)
    unit = jnp.where(lane - size == row, 1.0, 0.0).astype(F32)
    state = []
    for m in mats:
        full = jnp.where(lane < size, m, unit)
        state.append([full[b * 8 : b * 8 + 8] for b in range(size // 8)])
    sub = lax.broadcasted_iota(jnp.int32, (8, lanes), 0)
    pivots = [[jnp.ones((8, lanes), F32) for _ in range(size // 8)] for _ in mats]
    def spread(x):
        return jnp.broadcast_to(x, (8, lanes))

    for k in range(0, size, 2):
        first, s = k // 8, k % 8
        for i, blocks in enumerate(state):
            here = blocks[first]
            ones = [spread(blk[:, k : k + 1]) for blk in blocks[first:]]
            twos = [spread(blk[:, k + 1 : k + 2]) for blk in blocks[first:]]
            row_one, row_two = spread(here[s : s + 1, :]), spread(here[s + 1 : s + 2, :])
            a, below = spread(ones[0][s : s + 1, :]), spread(ones[0][s + 1 : s + 2, :])
            above, c = spread(twos[0][s : s + 1, :]), spread(twos[0][s + 1 : s + 2, :])
            inv_a = 1.0 / a
            ratio = above * inv_a
            d = c - below * ratio
            scaled_one = row_one * inv_a
            scaled_two = (row_two - below * scaled_one) * (1.0 / d)
            pivots[i][first] = jnp.where(
                sub == s, a, jnp.where(sub == s + 1, d, pivots[i][first])
            )
            for j, (one, two) in enumerate(zip(ones, twos)):
                two = two - one * ratio
                if j == 0:
                    one = jnp.where(sub > s, one, 0.0)
                    two = jnp.where(sub > s + 1, two, 0.0)
                blocks[first + j] = blocks[first + j] - one * scaled_one - two * scaled_two
    out = []
    for blocks, piv in zip(state, pivots):
        full = jnp.concatenate([blk * lax.rsqrt(p) for blk, p in zip(blocks, piv)], axis=0)
        out.append(right_half(full))
    return out


def scatter_a(cols, vec_ref, a_ref, ext, ext_low, own, reach):
    rows, slots = a_ref.shape[0], a_ref.shape[1]
    ext[...] = jnp.zeros_like(ext)
    for r in range(rows):
        y = vec_ref[r]
        for j in range(slots):
            c = cols[r * slots + j]
            ext[c] = ext[c] + low_dot(y, a_ref[r, j], NN)
    ext_low[...] = ext[...].astype(BF16)
    own[...] = ext[reach : reach + rows]


def me_index(nb):
    return lax.axis_index("dom") * nb + lax.axis_index("bal")


def place(t, nb):
    return (lax.div(t, nb), lax.rem(t, nb))


def strides(span):
    return [s for k in range(2, span + 1, 2) for s in (k, -k)]


def in_range(t, n):
    return jnp.logical_and(t >= 0, t < n)


def reaches(t, distance, span, n):
    return jnp.logical_and(in_range(t, n), jnp.abs(distance) <= span)


def toward_partner(me):
    return 1 - 2 * lax.rem(me, 2)


def neighbour_greet(barrier, me, n, nb, span):
    total = 1
    pl.semaphore_signal(
        barrier, inc=1, device_id=place(me + toward_partner(me), nb), device_id_type=MESH
    )
    for s in strides(span):
        ok = in_range(me + s, n)

        @pl.when(ok)
        def _(s=s):
            pl.semaphore_signal(barrier, inc=1, device_id=place(me + s, nb), device_id_type=MESH)

        total = total + ok.astype(jnp.int32)
    return total


def remote(src, dst, send, recv, target, nb):
    return pltpu.make_async_remote_copy(
        src_ref=src,
        dst_ref=dst,
        send_sem=send,
        recv_sem=recv,
        device_id=place(target, nb),
        device_id_type=MESH,
    )


class Window:
    def __init__(self, src, window, send, recv, psend, precv, me, n, nb, span):
        rows = src.shape[0]
        self.src, self.window, self.rows, self.span, self.me, self.n = src, window, rows, span, me, n
        go = toward_partner(me)
        partner = me + go
        self.own = remote(
            src, window.at[pl.ds((span - go) * rows, rows)], psend.at[span], precv.at[span], partner, nb
        )
        self.direct, self.relays = [], []
        for i, s in enumerate(strides(span)):
            here = window.at[pl.ds((span - s) * rows, rows)]
            copy = remote(src, here, send.at[i], recv.at[i], me + s, nb)
            self.direct.append((in_range(me + s, n), in_range(me - s, n), copy))
            give = reaches(me - s, s + go, span, n)
            get = reaches(partner - s, s - go, span, n)
            at = jnp.clip(span - s - go, 0, 2 * span) * rows
            relay = remote(
                here, window.at[pl.ds(at, rows)], psend.at[i], precv.at[i], partner, nb
            )
            self.relays.append((give, get, relay))

    def start(self):
        for ok, _, copy in self.direct:
            pl.when(ok)(copy.start)
        self.own.start()
        at = self.span * self.rows
        self.window[at : at + self.rows] = self.src[...]
        for s in range(-self.span, self.span + 1):
            if s != 0:

                @pl.when(jnp.logical_not(in_range(self.me - s, self.n)))
                def _(s=s):
                    at = (self.span - s) * self.rows
                    self.window[at : at + self.rows] = jnp.zeros(self.src.shape, self.window.dtype)

    def relay(self):
        for (_, arrives, copy), (give, _, relay) in zip(self.direct, self.relays):
            pl.when(arrives)(copy.wait_recv)
            pl.when(give)(relay.start)

    def finish(self):
        self.own.wait_recv()
        for _, get, relay in self.relays:
            pl.when(get)(relay.wait_recv)

    def sent(self):
        self.own.wait_send()
        for (ok, _, copy), (give, _, relay) in zip(self.direct, self.relays):
            pl.when(ok)(copy.wait_send)
            pl.when(give)(relay.wait_send)


class GiveBack:
    def __init__(self, ext, near, outgoing, landing, send, recv, psend, precv, me, n, nb, span, rows):
        self.ext, self.near, self.outgoing, self.landing = ext, near, outgoing, landing
        self.rows, self.span = rows, span
        go = toward_partner(me)
        partner = me + go
        self.own = remote(
            ext.at[pl.ds((span + go) * rows, rows)],
            near.at[span],
            psend.at[span],
            precv.at[span],
            partner,
            nb,
        )
        self.swaps, self.direct = [], []
        for i, s in enumerate(strides(span)):
            give = reaches(partner + s, s + go, span, n)
            get = reaches(me + s, s - go, span, n)
            at = jnp.clip(span + s + go, 0, 2 * span) * rows
            swap = remote(ext.at[pl.ds(at, rows)], near.at[i], psend.at[i], precv.at[i], partner, nb)
            self.swaps.append((give, get, swap))
            copy = remote(outgoing.at[i], landing.at[i], send.at[i], recv.at[i], me + s, nb)
            self.direct.append((in_range(me + s, n), in_range(me - s, n), copy))

    def start(self):
        for give, _, swap in self.swaps:
            pl.when(give)(swap.start)
        self.own.start()

    def forward(self):
        for i, s in enumerate(strides(self.span)):
            give, get, swap = self.swaps[i]
            ok, _, copy = self.direct[i]
            at = (self.span + s) * self.rows

            @pl.when(get)
            def _(i=i, at=at, swap=swap):
                swap.wait_recv()
                both = self.ext[at : at + self.rows].astype(F32) + self.near[i].astype(F32)
                self.outgoing[i] = both.astype(BF16)

            @pl.when(jnp.logical_not(get))
            def _(i=i, at=at):
                self.outgoing[i] = self.ext[at : at + self.rows]

            pl.when(ok)(copy.start)

    def finish(self, total):
        self.own.wait_recv()
        total[...] = total[...] + self.near[self.span].astype(F32)
        for i, (_, arrives, copy) in enumerate(self.direct):

            @pl.when(arrives)
            def _(i=i, copy=copy):
                copy.wait_recv()
                total[...] = total[...] + self.landing[i].astype(F32)

    def sent(self):
        self.own.wait_send()
        for (give, _, swap), (ok, _, copy) in zip(self.swaps, self.direct):
            pl.when(give)(swap.wait_send)
            pl.when(ok)(copy.wait_send)


def group_greet(barrier, dom, nb):
    d, b = lax.axis_index("dom"), lax.axis_index("bal")
    for o in range(1, nb):
        pl.semaphore_signal(
            barrier, inc=1, device_id=(d, lax.rem(b + o, nb)), device_id_type=MESH
        )
    for o in range(1, dom):
        pl.semaphore_signal(
            barrier, inc=1, device_id=(lax.rem(d + o, dom), b), device_id_type=MESH
        )
    return nb - 1 + dom - 1


def group_targets(dom, nb, axis):
    d, b = lax.axis_index("dom"), lax.axis_index("bal")
    if axis == "dom":
        return [(lax.rem(d + o, dom), b) for o in range(1, dom)]
    return [(d, lax.rem(b + o, nb)) for o in range(1, nb)]


class Reduce:
    def __init__(self, part, slots_b, mid, slots_d, whole, s1, r1, s2, r2, s3, r3, dom, nb):
        self.part, self.slots_b, self.mid, self.slots_d, self.whole = part, slots_b, mid, slots_d, whole
        self.place = lax.axis_index("bal")
        bal, far = group_targets(dom, nb, "bal"), group_targets(dom, nb, "dom")

        def copies(source, dest, targets, send, recv):
            return [
                pltpu.make_async_remote_copy(
                    src_ref=source(t),
                    dst_ref=dest(o),
                    send_sem=send.at[o],
                    recv_sem=recv.at[o],
                    device_id=t,
                    device_id_type=MESH,
                )
                for o, t in enumerate(targets)
            ]

        mine = whole.at[self.place]
        self.scatter = copies(lambda t: part.at[t[1]], lambda o: slots_b.at[o], bal, s1, r1)
        self.across = copies(lambda t: mid, lambda o: slots_d.at[o], far, s2, r2)
        self.gather = copies(lambda t: mine, lambda o: mine, bal, s3, r3)

    def start(self, value):
        count, height = self.part.shape[0], self.part.shape[1]
        for i in range(count):
            self.part[i] = value[i * height : (i + 1) * height]
        for copy in self.scatter:
            copy.start()

    def finish(self):
        total = self.part[self.place]
        for o, copy in enumerate(self.scatter):
            copy.wait_recv()
            total = total + self.slots_b[o]
        self.mid[...] = total
        for copy in self.across:
            copy.start()
        for o, copy in enumerate(self.across):
            copy.wait_recv()
            total = total + self.slots_d[o]
        self.whole[self.place] = total
        for copy in self.gather:
            copy.start()
        for copy in self.gather:
            copy.wait_recv()
        for copy in self.scatter + self.across + self.gather:
            copy.wait_send()
        return jnp.concatenate([self.whole[i] for i in range(self.whole.shape[0])], axis=0)


def reduce_scratch(height, lanes, dom, nb):
    dma = pltpu.SemaphoreType.DMA
    piece = height // nb
    return [
        pltpu.VMEM((nb, piece, lanes), F32),
        pltpu.VMEM((nb - 1, piece, lanes), F32),
        pltpu.VMEM((piece, lanes), F32),
        pltpu.VMEM((dom - 1, piece, lanes), F32),
        pltpu.VMEM((nb, piece, lanes), F32),
    ] + [dma((count - 1,)) for count in (nb, nb, dom, dom, nb, nb)]


def start_gram_kernel(dom, nb, x_ref, out_ref, *red):
    barrier = pltpu.get_barrier_semaphore()
    greeted = group_greet(barrier, dom, nb)
    reduce = Reduce(*red, dom, nb)
    x = wide(x_ref)
    value = dot3(x, beside(x, jnp.zeros_like(x)), NT)
    pl.semaphore_wait(barrier, greeted)
    reduce.start(value)
    out_ref[...] = reduce.finish()


def start_basis_kernel(
    total_rows, cols, gram_ref, x_ref, a_ref, basis, basis_low, ext_low, own, ext
):
    (inverse,) = inverse_factors([gram_ref[...] * (1.0 / total_rows)])
    value = dot3(inverse, wide(x_ref))
    put_wide(basis, value)
    put_wide(basis_low, value)
    scatter_a(cols, basis_low, a_ref, ext, ext_low, own, REACH_A)


def first_exchange_kernel(n, nb, basis_low, ext_low, own, window, back_low, total, *parts):
    rows = basis_low.shape[0]
    span_m, span_a = REACH_M // rows, REACH_A // rows
    me = me_index(nb)
    barrier = pltpu.get_barrier_semaphore()
    pl.semaphore_wait(barrier, neighbour_greet(barrier, me, n, nb, max(span_m, span_a)))
    fetch = Window(basis_low, window, *parts[:4], me, n, nb, span_m)
    give = GiveBack(ext_low, *parts[4:], me, n, nb, span_a, rows)
    give.start()
    fetch.start()
    give.forward()
    total[...] = own[...]
    fetch.relay()
    give.finish(total)
    back_low[...] = total[...].astype(BF16)
    fetch.finish()
    give.sent()
    fetch.sent()


def inverse_apply_kernel(
    group, row_ref, col_ref, count_ref, window, back_low, tiles, precond, precond_low, ext_low, own, ext
):
    rows = precond.shape[0]
    count = count_ref[0]
    precond[...] = jnp.zeros_like(precond)
    ext[...] = jnp.zeros_like(ext)

    def step(g, carry):
        for u in range(group):
            s = g * group + u
            r, c = row_ref[s], col_ref[s]
            live = s < count
            tile = tiles[s]
            ahead = low_dot(window[c], tile, NT)
            behind = low_dot(back_low[r], tile, NN)
            precond[r] = precond[r] + jnp.where(live, ahead, 0.0)
            ext[c] = ext[c] + jnp.where(live, behind, 0.0)
        return carry

    lax.fori_loop(0, lax.div(count + group - 1, group), step, 0)
    precond_low[...] = precond[...].astype(BF16)
    ext_low[...] = ext[...].astype(BF16)
    own[...] = ext[REACH_M : REACH_M + rows]


def second_exchange_kernel(
    n,
    dom,
    nb,
    total_rows,
    cols,
    precond_low,
    ext_low,
    own,
    a_ref,
    basis_ref,
    shadow_ref,
    residual_ref,
    image_out,
    u_out,
    s_out,
    mats,
    window,
    total,
    *parts,
):
    rows, slots = a_ref.shape[0], a_ref.shape[1]
    span_m, span_a = REACH_M // rows, REACH_A // rows
    me = me_index(nb)
    barrier = pltpu.get_barrier_semaphore()
    greeted = neighbour_greet(barrier, me, n, nb, max(span_m, span_a))
    pl.semaphore_wait(barrier, greeted + group_greet(barrier, dom, nb))
    fetch = Window(precond_low, window, *parts[:4], me, n, nb, span_a)
    give = GiveBack(ext_low, *parts[4:11], me, n, nb, span_m, rows)
    red = parts[11:]
    fetch.start()
    give.start()
    fetch.relay()
    give.forward()
    total[...] = own[...]
    fetch.finish()
    for r in range(rows):
        value = low_dot(window[cols[r * slots]], a_ref[r, 0], NT)
        for j in range(1, slots):
            value = value + low_dot(window[cols[r * slots + j]], a_ref[r, j], NT)
        image_out[r] = value
    image, shadow, residual = wide(image_out), wide(shadow_ref), wide(residual_ref)
    size = image.shape[0]
    left = lax.broadcasted_iota(jnp.int32, (size, 2 * size), 1) < size
    first = Reduce(*red[:11], dom, nb)
    crossed = dot3(beside(image, shadow), beside(image, shadow), NT)
    first.start(jnp.where(left, crossed[size:], crossed[:size]))
    target_t = dot3(residual, beside(image, image), NT)
    normal = jnp.where(left, crossed[:size], target_t)
    give.finish(total)
    both = first.finish() * (1.0 / total_rows)
    coupling, coupling_t = both[:, :size], right_half(both)
    u = image - dot3(coupling_t, wide(basis_ref))
    s = wide(total) - dot3(coupling, shadow)
    second = Reduce(*red[11:], dom, nb)
    news = beside(u, s)
    squares = dot3(news, news, NT)
    second.start(beside(jnp.where(left, squares[:size], squares[size:]), normal))
    put_wide(u_out, u)
    put_wide(s_out, s)
    mats[...] = second.finish()
    fetch.sent()
    give.sent()


def update_kernel(is_first, is_last, total_rows, cols, *refs):
    refs = list(refs)
    mats, image, u, s, precond, residual = refs[:6]
    refs = refs[6:]
    old = None if is_first else refs.pop(0)
    a_ref = None if is_last else refs.pop(0)
    solution_out, residual_out, basis, shadow = refs[:4]
    size = image.shape[1]
    grams = mats[:size, :] * (1.0 / total_rows)
    normal = mats[size:, :]
    inv_u, inv_s, inv_n = inverse_factors([grams, pltpu.roll(grams, size, 1), normal])
    weights_t = dot3(dot3(right_half(normal), inv_n, NT), inv_n)
    new_basis = dot3(inv_u, wide(u))
    put_wide(basis, new_basis)
    put_wide(shadow, dot3(inv_s, wide(s)))
    gained = dot3(weights_t, wide(precond))
    put_wide(solution_out, gained if is_first else wide(old) + gained)
    put_wide(residual_out, wide(residual) - dot3(weights_t, wide(image)))
    if not is_last:
        basis_low, ext_low, own, ext, shadow_low = refs[4:]
        put_wide(basis_low, new_basis)
        shadow_low[...] = shadow[...].astype(BF16)
        scatter_a(cols, shadow_low, a_ref, ext, ext_low, own, REACH_A)


def call(kernel, outs, args, scalars, scratch=(), collective=None):
    params = dict(vmem_limit_bytes=VMEM_BYTES)
    if collective is not None:
        params.update(collective_id=collective, has_side_effects=True)
    specs = [pl.BlockSpec(memory_space=pltpu.SMEM)] * scalars
    specs += [pl.BlockSpec(memory_space=pltpu.VMEM)] * (len(args) - scalars)
    return pl.pallas_call(
        kernel,
        out_shape=outs,
        in_specs=specs,
        out_specs=[pl.BlockSpec(memory_space=pltpu.VMEM)] * len(outs),
        scratch_shapes=list(scratch),
        compiler_params=pltpu.CompilerParams(**params),
    )(*args)


def shards(right_side, a_tiles, a_cols, m_tiles, m_rows, m_cols, m_count):
    rows, size, width = right_side.shape
    dom, nb = lax.axis_size("dom"), lax.axis_size("bal")
    n = dom * nb
    total_rows = rows * width * n
    span_a, span_m = REACH_A // rows, REACH_M // rows
    first_row = lax.axis_index(AXES) * rows
    a_win = (a_cols - first_row + REACH_A).reshape(-1)
    row_local = m_rows - first_row
    m_win = m_cols - first_row + REACH_M
    group = max(g for g in (8, 4, 2, 1) if m_tiles.shape[0] % g == 0)

    def shape(dtype, count=rows):
        return jax.ShapeDtypeStruct((count, size, width), dtype)

    high, low = shape(F32), shape(BF16)
    ext_a, ext_m = rows + 2 * REACH_A, rows + 2 * REACH_M
    dma = pltpu.SemaphoreType.DMA

    def sems(span):
        return [dma((span,)), dma((span,)), dma((span + 1,)), dma((span + 1,))]

    def give_scratch(span):
        return [
            pltpu.VMEM((count, rows, size, width), BF16) for count in (span + 1, span, span)
        ] + sems(span)

    (start,) = call(
        functools.partial(start_gram_kernel, dom, nb),
        [jax.ShapeDtypeStruct((size, 2 * size), F32)],
        [right_side],
        0,
        reduce_scratch(size, 2 * size, dom, nb),
        0,
    )
    basis, basis_low, given_a, own_a = call(
        functools.partial(start_basis_kernel, total_rows),
        [high, low, shape(BF16, ext_a), high],
        [a_win, start, right_side, a_tiles],
        1,
        [pltpu.VMEM((ext_a, size, width), F32)],
    )
    shadow, residual, solved = basis, right_side, None
    for iteration in range(ITERS):
        is_first, is_last = iteration == 0, iteration == ITERS - 1
        window, back_low = call(
            functools.partial(first_exchange_kernel, n, nb),
            [shape(BF16, ext_m), low],
            [basis_low, given_a, own_a],
            0,
            [pltpu.VMEM((rows, size, width), F32)] + sems(span_m) + give_scratch(span_a),
            1,
        )
        precond, precond_low, given_m, own_m = call(
            functools.partial(inverse_apply_kernel, group),
            [high, low, shape(BF16, ext_m), high],
            [row_local, m_win, m_count, window, back_low, m_tiles],
            3,
            [pltpu.VMEM((ext_m, size, width), F32)],
        )
        image, u, s, mats = call(
            functools.partial(second_exchange_kernel, n, dom, nb, total_rows),
            [high] * 3 + [jax.ShapeDtypeStruct((2 * size, 2 * size), F32)],
            [a_win, precond_low, given_m, own_m, a_tiles, basis, shadow, residual],
            1,
            [
                pltpu.VMEM((ext_a, size, width), BF16),
                pltpu.VMEM((rows, size, width), F32),
            ]
            + sems(span_a)
            + give_scratch(span_m)
            + reduce_scratch(size, 2 * size, dom, nb)
            + reduce_scratch(2 * size, 2 * size, dom, nb),
            2,
        )
        args = [a_win, mats, image, u, s, precond, residual]
        outs, scratch = [high] * 4, []
        if not is_first:
            args.append(solved)
        if not is_last:
            args.append(a_tiles)
            outs = outs + [low, shape(BF16, ext_a), high]
            scratch = [pltpu.VMEM((ext_a, size, width), F32), pltpu.VMEM((rows, size, width), BF16)]
        results = call(
            functools.partial(update_kernel, is_first, is_last, total_rows), outs, args, 1, scratch
        )
        solved, residual, basis, shadow = results[:4]
        if not is_last:
            basis_low, given_a, own_a = results[4:]
    return (solved, residual, basis, shadow)


def solution(mesh):
    vector = P(AXES, None, None)
    placed = (
        vector,
        P(AXES, None, None, None),
        P(AXES, None),
        P(AXES, None, None),
        P(AXES),
        P(AXES),
        P(AXES),
    )
    return jax.shard_map(
        shards, mesh=mesh, in_specs=placed, out_specs=(vector,) * 4, check_vma=False
    )
```
